32 devices in a mesh: sections: 2 (over x), chan: 16 (over z, y, core).
Axes of the slice: x: 2, y: 2, z: 4, core: 2. Of those that a mesh axis runs over, the one named last changes fastest.
Arguments:
- raw_field: bfloat16 [65536, 1024], P('chan', 'sections'), parts along dimension 1, may hold values from -12 to 12
- bin_list: int32 [128], replicated, may hold values from 1 to 1023, as said below
Outputs:
- cross_spectra: bfloat16 [1024, 512, 256], P(('sections', 'chan')), parts along dimension 0
The draws below stay inside these ranges and needn't reach their ends.
There are 2 independent parts, one for each index of `sections`. The reference program is written for one: setup_inputs(seed, part) draws one part's arguments, and reference() takes and returns one part's arrays. A program takes and returns all parts, laid end to end along the dimension named above; an argument that names none is the same for every part. Nothing has to cross between parts.
Inputs may be any that keep to these rules, and one draw needn't show every extreme that they name: `bin_list`: 128 distinct bin numbers in increasing order.
All inputs are finite; a program needn't handle non-finite values.
Results may differ from the reference program's by a relative error of at most 0.023.
Values may be sent and summed in bfloat16 or wider, within the bound.
A program may use at most 128 MiB of HBM per device.

```python
import math
import jax
import jax.numpy as jnp
import numpy as np
from jax import lax

C = 512
F = 128
L = 2048
RAW = 65536
N_CHAN = 16


def draw_bin_list(key, part):
    shuffled = jax.random.permutation(key, L // 2 - 3).astype(jnp.int32) + 2
    chosen = jnp.sort(shuffled[:F - 2])
    lowest = jnp.ones((1,), jnp.int32)
    highest = jnp.full((1,), L // 2 - 1, jnp.int32)
    return jnp.concatenate([lowest, chosen, highest])


def with_spikes(values, stream_key, source, target, shards_of, factor):
    def block_of(position):
        return (jnp.arange(values.shape[position]) // (values.shape[position] // shards_of)).reshape((-1,) + (1,) * (values.ndim - 1 - position))

    one_side = jax.random.permutation(stream_key, shards_of)[block_of(target)]
    other_side = (block_of(target) + shards_of // 2) % shards_of
    return jnp.where((block_of(source) == one_side) | (block_of(source) == other_side), factor * values, values)


def steps_of(stream_key, dims, split, least, high):
    factor_of = 1.0
    for position, blocks in split:
        steps = jax.random.uniform(jax.random.fold_in(jax.random.fold_in(stream_key, 6), position), (blocks,), jnp.float32, least / len(split), high / len(split))
        factor_of = factor_of * jnp.repeat(jnp.exp(steps), dims[position] // blocks).reshape((-1,) + (1,) * (len(dims) - 1 - position))
    return factor_of


def bell_draw_with(own_key, extent, width, bound, cuts, heavy, kind=jnp.bfloat16):
    result = width * jax.random.normal(own_key, extent, jnp.float32)
    if cuts:
        result = result * steps_of(own_key, extent, cuts, -0.22, 0.18)
    return jnp.clip(with_spikes(result, jax.random.fold_in(own_key, 3), *heavy), -bound, bound).astype(kind)


def setup_inputs(seed: int = 0, part: int = 0) -> dict:
    streams_of = jax.random.split(jax.random.key(seed), 3)
    own_keys = jax.random.split(jax.random.fold_in(streams_of[2], part), 3)
    return {
        "raw_field": bell_draw_with(own_keys[0], (RAW, C), 2.0, 12.0, ((0, 16),), (0, 1, 16, 2.0)),
        "bin_list": draw_bin_list(jax.random.fold_in(streams_of[2], 71), part),
    }


def lowpass_taps():
    shaped = []
    for offset in range(32):
        where = (offset - 15.5) / 4.0
        sinc_value = math.sin(math.pi * where) / (math.pi * where)
        hamming_value = 0.54 - 0.46 * math.cos(2.0 * math.pi * offset / 31.0)
        shaped.append(sinc_value * hamming_value)
    total = sum(shaped)
    return np.array([value / total for value in shaped], np.float32)


def hann_window(length):
    positions = jnp.arange(length, dtype=jnp.int32).astype(jnp.float32)
    return jnp.sin(math.pi * positions / length) ** 2


def window_power(length):
    return jnp.sum(hann_window(length) ** 2)


def fourier_table(bin_list, length):
    positions = jnp.arange(length, dtype=jnp.int32)
    phases = ((positions[:, None] * bin_list[None, :]) % length).astype(jnp.float32) * (2.0 * math.pi / length)
    window = hann_window(length)[:, None]
    cosines = window * jnp.cos(phases)
    sines = -window * jnp.sin(phases)
    half_len = length // 2
    leading = jnp.concatenate([cosines[:half_len], sines[:half_len]], 1)
    trailing = jnp.concatenate([cosines[half_len:], sines[half_len:]], 1)
    return jnp.concatenate([leading, trailing], 1).astype(jnp.bfloat16)


def decimate(padded, out_rows):
    filter_taps = lowpass_taps()
    summed = jnp.zeros((out_rows, padded.shape[1]), jnp.float32)
    for offset in range(32):
        row_start = 31 - offset
        picked = padded[row_start:row_start + 4 * out_rows:4]
        summed = summed + picked.astype(jnp.float32) * float(filter_taps[offset])
    return summed.astype(jnp.bfloat16)


def cross_parts(left_re, left_im, right_re, right_im):
    high = lax.Precision.HIGHEST

    def inner(first_op, second_op):
        return jnp.einsum("sif,sjf->ijf", first_op.astype(jnp.float32), second_op.astype(jnp.float32), precision=high)

    real_part = inner(left_re, right_re) + inner(left_im, right_im)
    imag_part = inner(left_im, right_re) - inner(left_re, right_im)
    return real_part, imag_part


def reference(raw_field, bin_list):
    total_rows, channels = raw_field.shape
    half_len = total_rows // (4 * N_CHAN)
    padded = jnp.concatenate([jnp.zeros((31, channels), raw_field.dtype), raw_field], 0)
    decimated = decimate(padded, total_rows // 4)
    fourier = fourier_table(bin_list, 2 * half_len)
    blocks = decimated.reshape(N_CHAN, half_len, channels)
    partial_value = jnp.einsum("bnc,nf->bcf", blocks.astype(jnp.float32), fourier.astype(jnp.float32), precision=lax.Precision.HIGHEST)
    bin_count = bin_list.shape[0]
    spectrum = (partial_value[:-1, :, :2 * bin_count] + partial_value[1:, :, 2 * bin_count:]).astype(jnp.bfloat16)
    spec_re = spectrum[..., :bin_count]
    spec_im = spectrum[..., bin_count:]
    real_part, imag_part = cross_parts(spec_re, spec_im, spec_re, spec_im)
    normalizer = 1.0 / ((N_CHAN - 1) * window_power(2 * half_len))
    return (jnp.concatenate([real_part, imag_part], 2) * normalizer).astype(jnp.bfloat16)
```

```python
import functools
import math

import jax
import jax.numpy as jnp
import numpy as np
from jax import lax
from jax.experimental import pallas as pl
from jax.experimental.pallas import tpu as pltpu
from jax.sharding import PartitionSpec as P

TAPS = 32
GROUP = 8
MESH = pl.DeviceIdType.MESH


def lowpass_taps():
    shaped = []
    for offset in range(TAPS):
        where = (offset - 15.5) / 4.0
        sinc_value = math.sin(math.pi * where) / (math.pi * where)
        hamming_value = 0.54 - 0.46 * math.cos(2.0 * math.pi * offset / 31.0)
        shaped.append(sinc_value * hamming_value)
    total = sum(shaped)
    return np.array([value / total for value in shaped], np.float64)


def band_matrix(out_rows):
    h = lowpass_taps()
    n = np.arange(out_rows)[:, None]
    m = np.arange(TAPS + 4 * out_rows)[None, :] - TAPS
    k = 4 * n - m
    inside = (k >= 0) & (k < TAPS)
    return np.where(inside, h[np.clip(k, 0, TAPS - 1)], 0.0)


def write_table(bins_ref, table_ref, half_len):
    length = 2 * half_len
    bin_count = bins_ref.shape[1]
    step = 2.0 * math.pi / length
    rows = jnp.broadcast_to(bins_ref[...].astype(jnp.float32), (128, bin_count))
    bins = jnp.transpose(rows).astype(jnp.int32)
    lane = lax.broadcasted_iota(jnp.int32, (bin_count, 128), 1)
    fine = (lax.rem(bins * lane, length)).astype(jnp.float32) * step
    coarse = (lax.rem(bins * lane * 128, length)).astype(jnp.float32) * step
    fine_cos, fine_sin = jnp.cos(fine), jnp.sin(fine)
    coarse_cos, coarse_sin = jnp.cos(coarse), jnp.sin(coarse)
    sign = 1.0 - 2.0 * lax.rem(bins, 2).astype(jnp.float32)

    def interleave(cosines, sines):
        pieces = []
        for g in range(bin_count // GROUP):
            pieces.append(cosines[g * GROUP : (g + 1) * GROUP])
            pieces.append(sines[g * GROUP : (g + 1) * GROUP])
        return jnp.concatenate(pieces, 0).astype(jnp.bfloat16)

    row_lane = lax.broadcasted_iota(jnp.int32, (8, 128), 1)
    for a in range(half_len // 128):
        ca, sa = coarse_cos[:, a : a + 1], coarse_sin[:, a : a + 1]
        cosines = fine_cos * ca - fine_sin * sa
        sines = -(fine_sin * ca + fine_cos * sa)
        position = (row_lane + a * 128).astype(jnp.float32) * (math.pi / length)
        leading = (jnp.sin(position) ** 2)[:1]
        trailing = (jnp.cos(position) ** 2)[:1] * sign
        columns = slice(a * 128, (a + 1) * 128)
        table_ref[0, :, columns] = interleave(cosines * leading, sines * leading)
        table_ref[1, :, columns] = interleave(cosines * trailing, sines * trailing)


def gather_kernel(
    n, raw_ref, bins_ref, band_ref, all_ref,
    raw_buf, table_ref, dec_ref, lead_ref, trail_out, trail_in, own_ref,
    raw_sem, halo_send, halo_recv, trail_send, trail_recv,
    own_sem, own_sib_send, own_sib_recv, ring_send, ring_recv, sib_send, sib_recv,
):
    chunks, _, width = raw_buf.shape
    raw_rows = raw_ref.shape[0]
    half_len = raw_rows // 4
    block = band_ref.shape[0]
    span = band_ref.shape[1]
    ring = n // 2
    me = lax.axis_index("chan")
    core = lax.rem(me, 2)
    chip = me // 2
    spot = jnp.where(lax.rem(chip, 2) == 0, chip // 2, ring - 1 - chip // 2)

    def device_at(position, which):
        position = lax.rem(position + 2 * ring, ring)
        at = jnp.where(position < ring // 2, 2 * position, 2 * (ring - 1 - position) + 1)
        return 2 * at + which

    sibling = 2 * chip + 1 - core
    neighbours = (device_at(spot + 1, core), device_at(spot - 1, core))
    after, before = lax.rem(me + 1, n), lax.rem(me + n - 1, n)

    def raw_copy(c):
        return pltpu.make_async_copy(
            raw_ref.at[:, pl.ds(c * width, width)],
            raw_buf.at[c, pl.ds(TAPS, raw_rows)],
            raw_sem.at[c],
        )

    def remote(src, dst, send, recv, target):
        return pltpu.make_async_remote_copy(
            src_ref=src, dst_ref=dst, send_sem=send, recv_sem=recv,
            device_id={"chan": target}, device_id_type=MESH,
        )

    for c in range(chunks):
        raw_copy(c).start()
    barrier = pltpu.get_barrier_semaphore()
    partners = neighbours + (sibling, after, before)
    for partner in partners:
        pl.semaphore_signal(barrier, inc=1, device_id={"chan": partner}, device_id_type=MESH)
    pl.semaphore_wait(barrier, len(partners))

    def halo_copy(c):
        return remote(
            raw_ref.at[pl.ds(raw_rows - TAPS, TAPS), pl.ds(c * width, width)],
            raw_buf.at[c, pl.ds(0, TAPS)],
            halo_send.at[c], halo_recv.at[c], after,
        )

    def trail_copy(c):
        return remote(trail_out.at[c], trail_in.at[c], trail_send.at[c], trail_recv.at[c], before)

    @pl.when(me < n - 1)
    def _():
        for c in range(chunks):
            halo_copy(c).start()

    @pl.when(me == 0)
    def _():
        for c in range(chunks):
            raw_buf[c, pl.ds(0, TAPS)] = jnp.zeros((TAPS, width), raw_buf.dtype)

    @pl.when(me == n - 1)
    def _():
        trail_in[...] = jnp.zeros(trail_in.shape, trail_in.dtype)

    write_table(bins_ref, table_ref, half_len)

    for c in range(chunks):
        raw_copy(c).wait()

        @pl.when(me > 0)
        def _():
            halo_copy(c).wait_recv()

        for b in range(half_len // block):
            dec_ref[pl.ds(b * block, block)] = jnp.dot(
                band_ref[...],
                raw_buf[c, pl.ds(b * 4 * block, span)],
                preferred_element_type=jnp.float32,
            ).astype(jnp.bfloat16)
        trail_out[c] = jnp.dot(
            table_ref[1], dec_ref[...], preferred_element_type=jnp.float32
        ).astype(jnp.bfloat16)

        @pl.when(me > 0)
        def _():
            trail_copy(c).start()

        lead_ref[c] = jnp.dot(table_ref[0], dec_ref[...], preferred_element_type=jnp.float32)

    reach = [[ring // 2 - (c % 2), ring // 2 - 1 + (c % 2)] for c in range(chunks)]

    def owner(way, t, which):
        return device_at(spot - t if way == 0 else spot + t, which)

    def ring_copy(way, c, t, src, whose):
        return remote(
            src, all_ref.at[whose, c],
            ring_send.at[way, c, t], ring_recv.at[way, c, t], neighbours[way],
        )

    def sib_copy(way, c, t, whose):
        return remote(
            all_ref.at[whose, c], all_ref.at[whose, c],
            sib_send.at[way, c, t], sib_recv.at[way, c, t], sibling,
        )

    def own_sib_copy(c, whose):
        return remote(
            own_ref.at[c], all_ref.at[whose, c], own_sib_send.at[c], own_sib_recv.at[c], sibling
        )

    def own_copy(c):
        return pltpu.make_async_copy(own_ref.at[c], all_ref.at[me, c], own_sem.at[c])

    for c in range(chunks):

        @pl.when(me < n - 1)
        def _():
            trail_copy(c).wait_recv()

        total = lead_ref[c] + trail_in[c].astype(jnp.float32)
        own_ref[c] = jnp.where(me < n - 1, total, 0.0).astype(jnp.bfloat16)
        for way in range(2):
            if reach[c][way] > 0:
                ring_copy(way, c, 0, own_ref.at[c], me).start()
        own_sib_copy(c, me).start()
        own_copy(c).start()

    for t in range(1, ring // 2 + 1):
        for c in range(chunks):
            for way in range(2):
                if t <= reach[c][way]:
                    whose = owner(way, t, core)
                    ring_copy(way, c, t - 1, own_ref.at[c], whose).wait_recv()
                    if t < reach[c][way]:
                        ring_copy(way, c, t, all_ref.at[whose, c], whose).start()
                    sib_copy(way, c, t - 1, whose).start()

    for c in range(chunks):

        @pl.when(me < n - 1)
        def _():
            halo_copy(c).wait_send()

        @pl.when(me > 0)
        def _():
            trail_copy(c).wait_send()

        own_copy(c).wait()
        own_sib_copy(c, me).wait_send()
        own_sib_copy(c, sibling).wait_recv()
        for way in range(2):
            for t in range(1, reach[c][way] + 1):
                if t == 1:
                    ring_copy(way, c, 0, own_ref.at[c], me).wait_send()
                else:
                    whose = owner(way, t - 1, core)
                    ring_copy(way, c, t - 1, all_ref.at[whose, c], whose).wait_send()
                sib_copy(way, c, t - 1, owner(way, t, core)).wait_send()
                sib_copy(way, c, t - 1, owner(way, t, 1 - core)).wait_recv()


def cross_kernel(n, scale, all_ref, out_ref, left_ref, flat_ref):
    tile = pl.program_id(0)
    rows = out_ref.shape[0]
    width = out_ref.shape[1]
    bins = out_ref.shape[2] // 2
    pair = 2 * GROUP
    groups = bins // GROUP
    depth = n * pair
    f32 = jnp.float32

    @pl.when(tile == 0)
    def _():
        first = lax.axis_index("chan") * rows
        mine = first // width
        chosen = (
            lax.broadcasted_iota(jnp.int32, (rows, width), 1)
            == lax.broadcasted_iota(jnp.int32, (rows, width), 0) + lax.rem(first, width)
        )
        chosen = jnp.where(chosen, 1.0, 0.0).astype(jnp.bfloat16)
        lane = lax.broadcasted_iota(jnp.int32, (rows, depth), 1)
        imag_lane = lax.rem(lane, pair) >= GROUP
        lane8 = lax.broadcasted_iota(jnp.int32, (GROUP, depth), 1)
        keep = jnp.where(
            lax.rem(lane8, GROUP) == lax.broadcasted_iota(jnp.int32, (GROUP, depth), 0), 1.0, 0.0
        )

        @pl.loop(0, groups)
        def _(g):
            at = pl.multiple_of(g * pair, pair)
            right = all_ref[:, mine, pl.ds(at, pair), :].reshape(depth, width)
            own = lax.dot_general(
                chosen, right, (((1,), (1,)), ((), ())), preferred_element_type=f32
            )
            turned = jnp.where(
                imag_lane, -pltpu.roll(own, GROUP, 1), pltpu.roll(own, depth - GROUP, 1)
            )
            for part, values in enumerate((own, turned)):
                spread = jnp.concatenate(
                    [jnp.broadcast_to(values[i : i + 1], (GROUP, depth)) * keep for i in range(rows)], 0
                )
                left_ref[g, pl.ds(part * rows * GROUP, rows * GROUP), :] = spread.astype(jnp.bfloat16)

    @pl.loop(0, groups)
    def _(g):
        at = pl.multiple_of(g * pair, pair)
        right = all_ref[:, tile, pl.ds(at, pair), :].reshape(depth, width)
        value = jnp.dot(left_ref[g], right, preferred_element_type=f32) * scale
        flat_ref[:, pl.ds(pl.multiple_of(g * GROUP, GROUP), GROUP), :] = value.reshape(
            2 * rows, GROUP, width
        )

    eye = (
        lax.broadcasted_iota(jnp.int32, (width, width), 0)
        == lax.broadcasted_iota(jnp.int32, (width, width), 1)
    )
    eye = jnp.where(eye, 1.0, 0.0).astype(jnp.bfloat16)

    @pl.loop(0, rows)
    def _(i):
        both = jnp.concatenate([flat_ref[i], flat_ref[rows + i]], 0).astype(jnp.bfloat16)
        out_ref[i] = lax.dot_general(
            eye, both, (((1,), (1,)), ((), ())), preferred_element_type=f32
        ).astype(jnp.bfloat16)


def per_device(n, raw_field, bin_list):
    raw_rows, channels = raw_field.shape
    bins = bin_list.shape[0]
    half_len = raw_rows // 4
    width = 256
    chunks = channels // width
    block = 128
    reach = n // 4
    bf16, f32 = jnp.bfloat16, jnp.float32
    band = jnp.asarray(band_matrix(block), bf16)
    dma = pltpu.SemaphoreType.DMA
    any_space = pl.BlockSpec(memory_space=pl.ANY)
    vmem = pl.BlockSpec(memory_space=pltpu.VMEM)
    gathered = pl.pallas_call(
        functools.partial(gather_kernel, n),
        out_shape=jax.ShapeDtypeStruct((n, chunks, 2 * bins, width), bf16),
        in_specs=[any_space, vmem, vmem],
        out_specs=any_space,
        scratch_shapes=[
            pltpu.VMEM((chunks, TAPS + raw_rows, width), bf16),
            pltpu.VMEM((2, 2 * bins, half_len), bf16),
            pltpu.VMEM((half_len, width), bf16),
            pltpu.VMEM((chunks, 2 * bins, width), f32),
            pltpu.VMEM((chunks, 2 * bins, width), bf16),
            pltpu.VMEM((chunks, 2 * bins, width), bf16),
            pltpu.VMEM((chunks, 2 * bins, width), bf16),
        ]
        + [dma((chunks,))] * 8
        + [dma((2, chunks, reach))] * 4,
        compiler_params=pltpu.CompilerParams(
            collective_id=0, has_side_effects=True, vmem_limit_bytes=40 * 2**20
        ),
        name="gather_spectra",
    )(raw_field, bin_list.reshape(1, bins), band)

    positions = np.arange(2 * half_len)
    power = float(np.sum(np.sin(np.pi * positions / (2 * half_len)) ** 4))
    rows = channels // n
    return pl.pallas_call(
        functools.partial(cross_kernel, n, 1.0 / ((n - 1) * power)),
        grid=(chunks,),
        out_shape=jax.ShapeDtypeStruct((rows, channels, 2 * bins), bf16),
        in_specs=[
            pl.BlockSpec(
                (n, chunks, 2 * bins, width), lambda j: (0, 0, 0, 0), pipeline_mode=pl.Buffered(1)
            )
        ],
        out_specs=pl.BlockSpec((rows, width, 2 * bins), lambda j: (0, j, 0)),
        scratch_shapes=[
            pltpu.VMEM((bins // GROUP, 2 * rows * GROUP, n * 2 * GROUP), bf16),
            pltpu.VMEM((2 * rows, bins, width), f32),
        ],
        compiler_params=pltpu.CompilerParams(vmem_limit_bytes=56 * 2**20),
        name="cross_products",
    )(gathered)


def solution(mesh):
    return jax.shard_map(
        functools.partial(per_device, mesh.shape["chan"]),
        mesh=mesh,
        in_specs=(P("chan", "sections"), P()),
        out_specs=P(("sections", "chan"), None, None),
        check_vma=False,
    )
```

```python
import functools
import math

import jax
import jax.numpy as jnp
import numpy as np
from jax import lax
from jax.experimental import pallas as pl
from jax.experimental.pallas import tpu as pltpu
from jax.sharding import PartitionSpec as P

TAPS = 32
GROUP = 8
MESH = pl.DeviceIdType.MESH


def lowpass_taps():
    shaped = []
    for offset in range(TAPS):
        where = (offset - 15.5) / 4.0
        sinc_value = math.sin(math.pi * where) / (math.pi * where)
        hamming_value = 0.54 - 0.46 * math.cos(2.0 * math.pi * offset / 31.0)
        shaped.append(sinc_value * hamming_value)
    total = sum(shaped)
    return np.array([value / total for value in shaped], np.float64)


def write_band(band_ref):
    rows, span = band_ref.shape
    taps = lowpass_taps()
    pieces = []
    for top in range(0, rows, 8):
        tiles = []
        for left in range(0, span, 128):
            wide = min(128, span - left)
            value = jnp.zeros((8, wide), jnp.float32)
            if left <= 4 * top + 60 and 4 * top + 1 < left + wide:
                row = lax.broadcasted_iota(jnp.int32, (8, wide), 0) + top
                column = lax.broadcasted_iota(jnp.int32, (8, wide), 1) + left
                offset = 4 * row + TAPS - column
                for k in range(TAPS):
                    value = jnp.where(offset == k, float(taps[k]), value)
            tiles.append(value)
        pieces.append(jnp.concatenate(tiles, 1))
    band_ref[...] = jnp.concatenate(pieces, 0).astype(band_ref.dtype)


def write_table(bins_ref, table_ref, half_len):
    length = 2 * half_len
    bin_count = bins_ref.shape[1]
    step = 2.0 * math.pi / length
    rows = jnp.broadcast_to(bins_ref[...].astype(jnp.float32), (128, bin_count))
    bins = jnp.transpose(rows).astype(jnp.int32)
    lane = lax.broadcasted_iota(jnp.int32, (bin_count, 128), 1)
    fine = (lax.rem(bins * lane, length)).astype(jnp.float32) * step
    coarse = (lax.rem(bins * lane * 128, length)).astype(jnp.float32) * step
    fine_cos, fine_sin = jnp.cos(fine), jnp.sin(fine)
    coarse_cos, coarse_sin = jnp.cos(coarse), jnp.sin(coarse)
    sign = 1.0 - 2.0 * lax.rem(bins, 2).astype(jnp.float32)

    def interleave(cosines, sines):
        pieces = []
        for g in range(bin_count // GROUP):
            pieces.append(cosines[g * GROUP : (g + 1) * GROUP])
            pieces.append(sines[g * GROUP : (g + 1) * GROUP])
        return jnp.concatenate(pieces, 0).astype(jnp.bfloat16)

    row_lane = lax.broadcasted_iota(jnp.int32, (8, 128), 1)
    for a in range(half_len // 128):
        ca, sa = coarse_cos[:, a : a + 1], coarse_sin[:, a : a + 1]
        cosines = fine_cos * ca - fine_sin * sa
        sines = -(fine_sin * ca + fine_cos * sa)
        position = (row_lane + a * 128).astype(jnp.float32) * (math.pi / length)
        leading = (jnp.sin(position) ** 2)[:1]
        trailing = (jnp.cos(position) ** 2)[:1] * sign
        columns = slice(a * 128, (a + 1) * 128)
        table_ref[0, :, columns] = interleave(cosines * leading, sines * leading)
        table_ref[1, :, columns] = interleave(cosines * trailing, sines * trailing)


def gather_kernel(
    n, raw_ref, bins_hbm, all_ref,
    raw_buf, bins_ref, band_ref, table_ref, dec_ref, lead_ref, trail_out, trail_in, own_ref,
    bins_sem, raw_sem, halo_send, halo_recv, trail_send, trail_recv,
    own_sem, own_sib_send, own_sib_recv, ring_send, ring_recv, sib_send, sib_recv,
):
    chunks, _, width = raw_buf.shape
    raw_rows = raw_ref.shape[0]
    half_len = raw_rows // 4
    block = band_ref.shape[0]
    span = band_ref.shape[1]
    ring = n // 2
    me = lax.axis_index("chan")
    core = lax.rem(me, 2)
    chip = me // 2
    spot = jnp.where(lax.rem(chip, 2) == 0, chip // 2, ring - 1 - chip // 2)

    def device_at(position, which):
        position = lax.rem(position + 2 * ring, ring)
        at = jnp.where(position < ring // 2, 2 * position, 2 * (ring - 1 - position) + 1)
        return 2 * at + which

    sibling = 2 * chip + 1 - core
    neighbours = (device_at(spot + 1, core), device_at(spot - 1, core))
    after, before = lax.rem(me + 1, n), lax.rem(me + n - 1, n)

    def raw_copy(c):
        return pltpu.make_async_copy(
            raw_ref.at[:, pl.ds(c * width, width)],
            raw_buf.at[c, pl.ds(TAPS, raw_rows)],
            raw_sem.at[c],
        )

    def remote(src, dst, send, recv, target):
        return pltpu.make_async_remote_copy(
            src_ref=src, dst_ref=dst, send_sem=send, recv_sem=recv,
            device_id={"chan": target}, device_id_type=MESH,
        )

    bins_copy = pltpu.make_async_copy(bins_hbm, bins_ref, bins_sem)
    bins_copy.start()
    for c in range(chunks):
        raw_copy(c).start()
    barrier = pltpu.get_barrier_semaphore()
    partners = neighbours + (sibling, after, before)
    for partner in partners:
        pl.semaphore_signal(barrier, inc=1, device_id={"chan": partner}, device_id_type=MESH)
    write_band(band_ref)
    pl.semaphore_wait(barrier, len(partners))

    def halo_copy(c):
        return remote(
            raw_ref.at[pl.ds(raw_rows - TAPS, TAPS), pl.ds(c * width, width)],
            raw_buf.at[c, pl.ds(0, TAPS)],
            halo_send.at[c], halo_recv.at[c], after,
        )

    def trail_copy(c):
        return remote(trail_out.at[c], trail_in.at[c], trail_send.at[c], trail_recv.at[c], before)

    @pl.when(me < n - 1)
    def _():
        for c in range(chunks):
            halo_copy(c).start()

    @pl.when(me == 0)
    def _():
        for c in range(chunks):
            raw_buf[c, pl.ds(0, TAPS)] = jnp.zeros((TAPS, width), raw_buf.dtype)

    @pl.when(me == n - 1)
    def _():
        trail_in[...] = jnp.zeros(trail_in.shape, trail_in.dtype)

    bins_copy.wait()
    write_table(bins_ref, table_ref, half_len)

    for c in range(chunks):
        raw_copy(c).wait()

        @pl.when(me > 0)
        def _():
            halo_copy(c).wait_recv()

        for b in range(half_len // block):
            dec_ref[pl.ds(b * block, block)] = jnp.dot(
                band_ref[...],
                raw_buf[c, pl.ds(b * 4 * block, span)],
                preferred_element_type=jnp.float32,
            ).astype(jnp.bfloat16)
        trail_out[c] = jnp.dot(
            table_ref[1], dec_ref[...], preferred_element_type=jnp.float32
        ).astype(jnp.bfloat16)

        @pl.when(me > 0)
        def _():
            trail_copy(c).start()

        lead_ref[c] = jnp.dot(table_ref[0], dec_ref[...], preferred_element_type=jnp.float32)

    reach = [[ring // 2 - (c % 2), ring // 2 - 1 + (c % 2)] for c in range(chunks)]

    def owner(way, t, which):
        return device_at(spot - t if way == 0 else spot + t, which)

    def ring_copy(way, c, t, src, whose):
        return remote(
            src, all_ref.at[whose, c],
            ring_send.at[way, c, t], ring_recv.at[way, c, t], neighbours[way],
        )

    def sib_copy(way, c, t, whose):
        return remote(
            all_ref.at[whose, c], all_ref.at[whose, c],
            sib_send.at[way, c, t], sib_recv.at[way, c, t], sibling,
        )

    def own_sib_copy(c, whose):
        return remote(
            own_ref.at[c], all_ref.at[whose, c], own_sib_send.at[c], own_sib_recv.at[c], sibling
        )

    def own_copy(c):
        return pltpu.make_async_copy(own_ref.at[c], all_ref.at[me, c], own_sem.at[c])

    for c in range(chunks):

        @pl.when(me < n - 1)
        def _():
            trail_copy(c).wait_recv()

        total = lead_ref[c] + trail_in[c].astype(jnp.float32)
        own_ref[c] = jnp.where(me < n - 1, total, 0.0).astype(jnp.bfloat16)
        for way in range(2):
            if reach[c][way] > 0:
                ring_copy(way, c, 0, own_ref.at[c], me).start()
        own_sib_copy(c, me).start()
        own_copy(c).start()

    for t in range(1, ring // 2 + 1):
        for c in range(chunks):
            for way in range(2):
                if t <= reach[c][way]:
                    whose = owner(way, t, core)
                    ring_copy(way, c, t - 1, own_ref.at[c], whose).wait_recv()
                    if t < reach[c][way]:
                        ring_copy(way, c, t, all_ref.at[whose, c], whose).start()
                    sib_copy(way, c, t - 1, whose).start()

    for c in range(chunks):

        @pl.when(me < n - 1)
        def _():
            halo_copy(c).wait_send()

        @pl.when(me > 0)
        def _():
            trail_copy(c).wait_send()

        own_copy(c).wait()
        own_sib_copy(c, me).wait_send()
        own_sib_copy(c, sibling).wait_recv()
        for way in range(2):
            for t in range(1, reach[c][way] + 1):
                if t == 1:
                    ring_copy(way, c, 0, own_ref.at[c], me).wait_send()
                else:
                    whose = owner(way, t - 1, core)
                    ring_copy(way, c, t - 1, all_ref.at[whose, c], whose).wait_send()
                sib_copy(way, c, t - 1, owner(way, t, core)).wait_send()
                sib_copy(way, c, t - 1, owner(way, t, 1 - core)).wait_recv()


def cross_kernel(n, scale, all_ref, out_ref, left_ref, flat_ref, stage_ref, out_sem):
    rows = out_ref.shape[0]
    chunks, width = all_ref.shape[1], all_ref.shape[3]
    bins = out_ref.shape[2] // 2
    pair = 2 * GROUP
    groups = bins // GROUP
    depth = n * pair
    f32 = jnp.float32

    first = lax.axis_index("chan") * rows
    mine = first // width
    chosen = (
        lax.broadcasted_iota(jnp.int32, (rows, width), 1)
        == lax.broadcasted_iota(jnp.int32, (rows, width), 0) + lax.rem(first, width)
    )
    chosen = jnp.where(chosen, 1.0, 0.0).astype(jnp.bfloat16)
    imag_lane = lax.rem(lax.broadcasted_iota(jnp.int32, (rows, depth), 1), pair) >= GROUP
    lane8 = lax.broadcasted_iota(jnp.int32, (GROUP, depth), 1)
    keep = lax.rem(lane8, GROUP) == lax.broadcasted_iota(jnp.int32, (GROUP, depth), 0)
    keep = jnp.where(keep, 1.0, 0.0)

    @pl.loop(0, groups, unroll=4)
    def _(g):
        at = pl.multiple_of(g * pair, pair)
        own = lax.dot_general(
            chosen,
            all_ref[:, mine, pl.ds(at, pair), :].reshape(depth, width),
            (((1,), (1,)), ((), ())),
            preferred_element_type=f32,
        )
        turned = jnp.where(
            imag_lane, -pltpu.roll(own, GROUP, 1), pltpu.roll(own, depth - GROUP, 1)
        )
        for part, values in enumerate((own, turned)):
            spread = jnp.concatenate(
                [jnp.broadcast_to(values[i : i + 1], (GROUP, depth)) * keep for i in range(rows)], 0
            )
            left_ref[g, pl.ds(part * rows * GROUP, rows * GROUP), :] = spread.astype(jnp.bfloat16)
        right = jnp.concatenate(
            [all_ref[:, c, pl.ds(at, pair), :].reshape(depth, width) for c in range(chunks)], 1
        )
        value = jnp.dot(left_ref[g], right, preferred_element_type=f32) * scale
        flat_ref[:, pl.ds(pl.multiple_of(g * GROUP, GROUP), GROUP), :] = value.reshape(
            2 * rows, GROUP, chunks * width
        )

    def out_copy(i):
        return pltpu.make_async_copy(stage_ref.at[i], out_ref.at[i], out_sem.at[i])

    @pl.loop(0, rows, unroll=4)
    def _(i):
        both = jnp.concatenate([flat_ref[i], flat_ref[rows + i]], 0).astype(jnp.bfloat16)
        stage_ref[i] = both.T
        out_copy(i).start()

    @pl.loop(0, rows)
    def _(i):
        out_copy(i).wait()


def per_device(n, raw_field, bin_list):
    raw_rows, channels = raw_field.shape
    bins = bin_list.shape[0]
    half_len = raw_rows // 4
    width = 256
    chunks = channels // width
    block = 128
    reach = n // 4
    bf16, f32 = jnp.bfloat16, jnp.float32
    dma = pltpu.SemaphoreType.DMA
    hbm = pl.BlockSpec(memory_space=pltpu.HBM)
    vmem = pl.BlockSpec(memory_space=pltpu.VMEM)
    gathered = pl.pallas_call(
        functools.partial(gather_kernel, n),
        out_shape=jax.ShapeDtypeStruct((n, chunks, 2 * bins, width), bf16),
        in_specs=[hbm, hbm],
        out_specs=vmem,
        scratch_shapes=[
            pltpu.VMEM((chunks, TAPS + raw_rows, width), bf16),
            pltpu.VMEM((1, bins), jnp.int32),
            pltpu.VMEM((block, TAPS + 4 * block), bf16),
            pltpu.VMEM((2, 2 * bins, half_len), bf16),
            pltpu.VMEM((half_len, width), bf16),
            pltpu.VMEM((chunks, 2 * bins, width), f32),
            pltpu.VMEM((chunks, 2 * bins, width), bf16),
            pltpu.VMEM((chunks, 2 * bins, width), bf16),
            pltpu.VMEM((chunks, 2 * bins, width), bf16),
        ]
        + [dma]
        + [dma((chunks,))] * 8
        + [dma((2, chunks, reach))] * 4,
        compiler_params=pltpu.CompilerParams(
            collective_id=0,
            has_side_effects=True,
            vmem_limit_bytes=50 * 2**20 - n * channels * 2 * bins * 2,
        ),
        name="gather_spectra",
    )(raw_field, bin_list.reshape(1, bins))

    positions = np.arange(2 * half_len)
    power = float(np.sum(np.sin(np.pi * positions / (2 * half_len)) ** 4))
    rows = channels // n
    return pl.pallas_call(
        functools.partial(cross_kernel, n, 1.0 / ((n - 1) * power)),
        out_shape=jax.ShapeDtypeStruct((rows, channels, 2 * bins), bf16),
        in_specs=[vmem],
        out_specs=hbm,
        scratch_shapes=[
            pltpu.VMEM((bins // GROUP, 2 * rows * GROUP, n * 2 * GROUP), bf16),
            pltpu.VMEM((2 * rows, bins, channels), f32),
            pltpu.VMEM((rows, channels, 2 * bins), bf16),
            dma((rows,)),
        ],
        compiler_params=pltpu.CompilerParams(vmem_limit_bytes=40 * 2**20),
        name="cross_products",
    )(gathered)


def solution(mesh):
    return jax.shard_map(
        functools.partial(per_device, mesh.shape["chan"]),
        mesh=mesh,
        in_specs=(P("chan", "sections"), P()),
        out_specs=P(("sections", "chan"), None, None),
        check_vma=False,
    )
```

```python
import functools
import math

import jax
import jax.numpy as jnp
import numpy as np
from jax import lax
from jax.experimental import pallas as pl
from jax.experimental.pallas import tpu as pltpu
from jax.sharding import PartitionSpec as P

TAPS = 32
GROUP = 8
MESH = pl.DeviceIdType.MESH


def lowpass_taps():
    shaped = []
    for offset in range(TAPS):
        where = (offset - 15.5) / 4.0
        sinc_value = math.sin(math.pi * where) / (math.pi * where)
        hamming_value = 0.54 - 0.46 * math.cos(2.0 * math.pi * offset / 31.0)
        shaped.append(sinc_value * hamming_value)
    total = sum(shaped)
    return np.array([value / total for value in shaped], np.float64)


def write_band(band_ref):
    rows, span = band_ref.shape
    taps = lowpass_taps()
    pieces = []
    for top in range(0, rows, 8):
        tiles = []
        for left in range(0, span, 128):
            wide = min(128, span - left)
            value = jnp.zeros((8, wide), jnp.float32)
            if left <= 4 * top + 60 and 4 * top + 1 < left + wide:
                row = lax.broadcasted_iota(jnp.int32, (8, wide), 0) + top
                column = lax.broadcasted_iota(jnp.int32, (8, wide), 1) + left
                offset = 4 * row + TAPS - column
                for k in range(TAPS):
                    value = jnp.where(offset == k, float(taps[k]), value)
            tiles.append(value)
        pieces.append(jnp.concatenate(tiles, 1))
    band_ref[...] = jnp.concatenate(pieces, 0).astype(band_ref.dtype)


def write_table(bins_ref, table_ref, half_len):
    length = 2 * half_len
    bin_count = bins_ref.shape[1]
    step = 2.0 * math.pi / length
    rows = jnp.broadcast_to(bins_ref[...].astype(jnp.float32), (128, bin_count))
    bins = jnp.transpose(rows).astype(jnp.int32)
    lane = lax.broadcasted_iota(jnp.int32, (bin_count, 128), 1)
    fine = (lax.rem(bins * lane, length)).astype(jnp.float32) * step
    coarse = (lax.rem(bins * lane * 128, length)).astype(jnp.float32) * step
    fine_cos, fine_sin = jnp.cos(fine), jnp.sin(fine)
    coarse_cos, coarse_sin = jnp.cos(coarse), jnp.sin(coarse)
    sign = 1.0 - 2.0 * lax.rem(bins, 2).astype(jnp.float32)

    def interleave(cosines, sines):
        pieces = []
        for g in range(bin_count // GROUP):
            pieces.append(cosines[g * GROUP : (g + 1) * GROUP])
            pieces.append(sines[g * GROUP : (g + 1) * GROUP])
        return jnp.concatenate(pieces, 0).astype(jnp.bfloat16)

    row_lane = lax.broadcasted_iota(jnp.int32, (8, 128), 1)
    for a in range(half_len // 128):
        ca, sa = coarse_cos[:, a : a + 1], coarse_sin[:, a : a + 1]
        cosines = fine_cos * ca - fine_sin * sa
        sines = -(fine_sin * ca + fine_cos * sa)
        position = (row_lane + a * 128).astype(jnp.float32) * (math.pi / length)
        leading = (jnp.sin(position) ** 2)[:1]
        trailing = (jnp.cos(position) ** 2)[:1] * sign
        columns = slice(a * 128, (a + 1) * 128)
        table_ref[0, :, columns] = interleave(cosines * leading, sines * leading)
        table_ref[1, :, columns] = interleave(cosines * trailing, sines * trailing)


def gather_kernel(
    n, raw_ref, bins_hbm, all_ref,
    raw_buf, bins_ref, band_ref, table_ref, dec_ref, lead_ref, trail_out, trail_in, own_ref,
    bins_sem, raw_sem, halo_send, halo_recv, trail_send, trail_recv,
    own_sem, own_sib_send, own_sib_recv, ring_send, ring_recv, sib_send, sib_recv,
):
    chunks, _, width = raw_buf.shape
    raw_rows = raw_ref.shape[0]
    half_len = raw_rows // 4
    block = band_ref.shape[0]
    span = band_ref.shape[1]
    ring = n // 2
    me = lax.axis_index("chan")
    core = lax.rem(me, 2)
    chip = me // 2
    spot = jnp.where(lax.rem(chip, 2) == 0, chip // 2, ring - 1 - chip // 2)

    def device_at(position, which):
        position = lax.rem(position + 2 * ring, ring)
        at = jnp.where(position < ring // 2, 2 * position, 2 * (ring - 1 - position) + 1)
        return 2 * at + which

    sibling = 2 * chip + 1 - core
    neighbours = (device_at(spot + 1, core), device_at(spot - 1, core))
    after, before = lax.rem(me + 1, n), lax.rem(me + n - 1, n)

    def raw_copy(c):
        return pltpu.make_async_copy(
            raw_ref.at[:, pl.ds(c * width, width)],
            raw_buf.at[c, pl.ds(TAPS, raw_rows)],
            raw_sem.at[c],
        )

    def remote(src, dst, send, recv, target):
        return pltpu.make_async_remote_copy(
            src_ref=src, dst_ref=dst, send_sem=send, recv_sem=recv,
            device_id={"chan": target}, device_id_type=MESH,
        )

    bins_copy = pltpu.make_async_copy(bins_hbm, bins_ref, bins_sem)
    bins_copy.start()
    for c in range(chunks):
        raw_copy(c).start()
    barrier = pltpu.get_barrier_semaphore()
    partners = neighbours + (sibling, after, before)
    for partner in partners:
        pl.semaphore_signal(barrier, inc=1, device_id={"chan": partner}, device_id_type=MESH)
    write_band(band_ref)
    pl.semaphore_wait(barrier, len(partners))

    def halo_copy(c):
        return remote(
            raw_ref.at[pl.ds(raw_rows - TAPS, TAPS), pl.ds(c * width, width)],
            raw_buf.at[c, pl.ds(0, TAPS)],
            halo_send.at[c], halo_recv.at[c], after,
        )

    def trail_copy(c):
        return remote(trail_out.at[c], trail_in.at[c], trail_send.at[c], trail_recv.at[c], before)

    @pl.when(me < n - 1)
    def _():
        for c in range(chunks):
            halo_copy(c).start()

    @pl.when(me == 0)
    def _():
        for c in range(chunks):
            raw_buf[c, pl.ds(0, TAPS)] = jnp.zeros((TAPS, width), raw_buf.dtype)

    @pl.when(me == n - 1)
    def _():
        trail_in[...] = jnp.zeros(trail_in.shape, trail_in.dtype)

    bins_copy.wait()
    write_table(bins_ref, table_ref, half_len)

    for c in range(chunks):
        raw_copy(c).wait()

        @pl.when(me > 0)
        def _():
            halo_copy(c).wait_recv()

        for b in range(half_len // block):
            dec_ref[pl.ds(b * block, block)] = jnp.dot(
                band_ref[...],
                raw_buf[c, pl.ds(b * 4 * block, span)],
                preferred_element_type=jnp.float32,
            ).astype(jnp.bfloat16)
        trail_out[c] = jnp.dot(
            table_ref[1], dec_ref[...], preferred_element_type=jnp.float32
        ).astype(jnp.bfloat16)

        @pl.when(me > 0)
        def _():
            trail_copy(c).start()

        lead_ref[c] = jnp.dot(table_ref[0], dec_ref[...], preferred_element_type=jnp.float32)

    reach = [[ring // 2 - (c % 2), ring // 2 - 1 + (c % 2)] for c in range(chunks)]

    def owner(way, t, which):
        return device_at(spot - t if way == 0 else spot + t, which)

    def ring_copy(way, c, t, src, whose):
        return remote(
            src, all_ref.at[whose, c],
            ring_send.at[way, c, t], ring_recv.at[way, c, t], neighbours[way],
        )

    def sib_copy(way, c, t, whose):
        return remote(
            all_ref.at[whose, c], all_ref.at[whose, c],
            sib_send.at[way, c, t], sib_recv.at[way, c, t], sibling,
        )

    def own_sib_copy(c, whose):
        return remote(
            own_ref.at[c], all_ref.at[whose, c], own_sib_send.at[c], own_sib_recv.at[c], sibling
        )

    def own_copy(c):
        return pltpu.make_async_copy(own_ref.at[c], all_ref.at[me, c], own_sem.at[c])

    for c in range(chunks):

        @pl.when(me < n - 1)
        def _():
            trail_copy(c).wait_recv()

        total = lead_ref[c] + trail_in[c].astype(jnp.float32)
        own_ref[c] = jnp.where(me < n - 1, total, 0.0).astype(jnp.bfloat16)
        for way in range(2):
            if reach[c][way] > 0:
                ring_copy(way, c, 0, own_ref.at[c], me).start()
        own_sib_copy(c, me).start()
        own_copy(c).start()

    for t in range(1, ring // 2 + 1):
        for c in range(chunks):
            for way in range(2):
                if t <= reach[c][way]:
                    whose = owner(way, t, core)
                    ring_copy(way, c, t - 1, own_ref.at[c], whose).wait_recv()
                    if t < reach[c][way]:
                        ring_copy(way, c, t, all_ref.at[whose, c], whose).start()
                    sib_copy(way, c, t - 1, whose).start()

    for c in range(chunks):

        @pl.when(me < n - 1)
        def _():
            halo_copy(c).wait_send()

        @pl.when(me > 0)
        def _():
            trail_copy(c).wait_send()

        own_copy(c).wait()
        own_sib_copy(c, me).wait_send()
        own_sib_copy(c, sibling).wait_recv()
        for way in range(2):
            for t in range(1, reach[c][way] + 1):
                if t == 1:
                    ring_copy(way, c, 0, own_ref.at[c], me).wait_send()
                else:
                    whose = owner(way, t - 1, core)
                    ring_copy(way, c, t - 1, all_ref.at[whose, c], whose).wait_send()
                sib_copy(way, c, t - 1, owner(way, t, core)).wait_send()
                sib_copy(way, c, t - 1, owner(way, t, 1 - core)).wait_recv()


def cross_kernel(n, scale, all_ref, out_ref, left_ref, flat_ref, stage_ref, out_sem):
    rows = out_ref.shape[0]
    chunks, width = all_ref.shape[1], all_ref.shape[3]
    bins = out_ref.shape[2] // 2
    pair = 2 * GROUP
    groups = bins // GROUP
    depth = n * pair
    f32 = jnp.float32

    first = lax.axis_index("chan") * rows
    mine = first // width
    chosen = (
        lax.broadcasted_iota(jnp.int32, (rows, width), 1)
        == lax.broadcasted_iota(jnp.int32, (rows, width), 0) + lax.rem(first, width)
    )
    chosen = jnp.where(chosen, 1.0, 0.0).astype(jnp.bfloat16)
    imag_lane = lax.rem(lax.broadcasted_iota(jnp.int32, (rows, depth), 1), pair) >= GROUP
    lane8 = lax.broadcasted_iota(jnp.int32, (GROUP, depth), 1)
    keep = lax.rem(lane8, GROUP) == lax.broadcasted_iota(jnp.int32, (GROUP, depth), 0)
    keep = jnp.where(keep, 1.0, 0.0)

    @pl.loop(0, groups, unroll=16)
    def _(g):
        at = pl.multiple_of(g * pair, pair)
        own = lax.dot_general(
            chosen,
            all_ref[:, mine, pl.ds(at, pair), :].reshape(depth, width),
            (((1,), (1,)), ((), ())),
            preferred_element_type=f32,
        )
        turned = jnp.where(
            imag_lane, -pltpu.roll(own, GROUP, 1), pltpu.roll(own, depth - GROUP, 1)
        )
        for part, values in enumerate((own, turned)):
            spread = jnp.concatenate(
                [jnp.broadcast_to(values[i : i + 1], (GROUP, depth)) * keep for i in range(rows)], 0
            )
            left_ref[g, pl.ds(part * rows * GROUP, rows * GROUP), :] = spread.astype(jnp.bfloat16)
        right = jnp.concatenate(
            [all_ref[:, c, pl.ds(at, pair), :].reshape(depth, width) for c in range(chunks)], 1
        )
        value = jnp.dot(left_ref[g], right, preferred_element_type=f32) * scale
        flat_ref[:, pl.ds(pl.multiple_of(g * GROUP, GROUP), GROUP), :] = value.reshape(
            2 * rows, GROUP, chunks * width
        )

    def out_copy(i):
        return pltpu.make_async_copy(stage_ref.at[i], out_ref.at[i], out_sem.at[i])

    @pl.loop(0, rows, unroll=min(rows, 16))
    def _(i):
        both = jnp.concatenate([flat_ref[i], flat_ref[rows + i]], 0).astype(jnp.bfloat16)
        stage_ref[i] = both.T
        out_copy(i).start()

    @pl.loop(0, rows)
    def _(i):
        out_copy(i).wait()


def per_device(n, raw_field, bin_list):
    raw_rows, channels = raw_field.shape
    bins = bin_list.shape[0]
    half_len = raw_rows // 4
    width = 256
    chunks = channels // width
    block = 128
    reach = n // 4
    bf16, f32 = jnp.bfloat16, jnp.float32
    dma = pltpu.SemaphoreType.DMA
    hbm = pl.BlockSpec(memory_space=pltpu.HBM)
    vmem = pl.BlockSpec(memory_space=pltpu.VMEM)
    gathered = pl.pallas_call(
        functools.partial(gather_kernel, n),
        out_shape=jax.ShapeDtypeStruct((n, chunks, 2 * bins, width), bf16),
        in_specs=[hbm, hbm],
        out_specs=vmem,
        scratch_shapes=[
            pltpu.VMEM((chunks, TAPS + raw_rows, width), bf16),
            pltpu.VMEM((1, bins), jnp.int32),
            pltpu.VMEM((block, TAPS + 4 * block), bf16),
            pltpu.VMEM((2, 2 * bins, half_len), bf16),
            pltpu.VMEM((half_len, width), bf16),
            pltpu.VMEM((chunks, 2 * bins, width), f32),
            pltpu.VMEM((chunks, 2 * bins, width), bf16),
            pltpu.VMEM((chunks, 2 * bins, width), bf16),
            pltpu.VMEM((chunks, 2 * bins, width), bf16),
        ]
        + [dma]
        + [dma((chunks,))] * 8
        + [dma((2, chunks, reach))] * 4,
        compiler_params=pltpu.CompilerParams(
            collective_id=0,
            has_side_effects=True,
            vmem_limit_bytes=50 * 2**20 - n * channels * 2 * bins * 2,
        ),
        name="gather_spectra",
    )(raw_field, bin_list.reshape(1, bins))

    positions = np.arange(2 * half_len)
    power = float(np.sum(np.sin(np.pi * positions / (2 * half_len)) ** 4))
    rows = channels // n
    return pl.pallas_call(
        functools.partial(cross_kernel, n, 1.0 / ((n - 1) * power)),
        out_shape=jax.ShapeDtypeStruct((rows, channels, 2 * bins), bf16),
        in_specs=[vmem],
        out_specs=hbm,
        scratch_shapes=[
            pltpu.VMEM((bins // GROUP, 2 * rows * GROUP, n * 2 * GROUP), bf16),
            pltpu.VMEM((2 * rows, bins, channels), f32),
            pltpu.VMEM((rows, channels, 2 * bins), bf16),
            dma((rows,)),
        ],
        compiler_params=pltpu.CompilerParams(vmem_limit_bytes=40 * 2**20),
        name="cross_products",
    )(gathered)


def solution(mesh):
    return jax.shard_map(
        functools.partial(per_device, mesh.shape["chan"]),
        mesh=mesh,
        in_specs=(P("chan", "sections"), P()),
        out_specs=P(("sections", "chan"), None, None),
        check_vma=False,
    )
```
